32 devices in a mesh: ctx: 4 (over z), exp: 8 (over y, x, core).
Axes of the slice: x: 2, y: 2, z: 4, core: 2. Of those that a mesh axis runs over, the one named last changes fastest.
Arguments:
- query_rows: bfloat16 [768, 1024], P('ctx', 'exp'), may hold values from -6 to 6
- key_rows: bfloat16 [768, 1024], P('ctx', 'exp'), may hold values from -6 to 6
- value_rows: bfloat16 [768, 1024], P('ctx', 'exp'), may hold values from -6 to 6
- log_decay: float32 [8, 768], P('exp', 'ctx'), may hold values from -1 to 0
- residual: bfloat16 [768, 3072], P(('ctx', 'exp')), may hold values from -20 to 20
- norm_gain: float32 [3072], replicated, may hold values from 0.1 to 1.9
- out_grad: bfloat16 [768, 3072], P(('ctx', 'exp')), may hold values from -6 to 6
- experts_of: int32 [768, 2], P(('ctx', 'exp')), may hold values from 0 to 7, all different within a row; in each aligned block of 24 rows (0 to 23, 24 to 47, ...) at most 9 rows name the same one
- route_weight: float32 [768, 2], P(('ctx', 'exp')), may hold values from 0.1 to 0.9
- output_weight: bfloat16 [1024, 3072], P('exp'), may hold values from -0.1875 to 0.1875
- expert_gate: bfloat16 [8, 3072, 4608], P('exp', None, 'ctx'), may hold values from -0.109375 to 0.109375
- expert_up: bfloat16 [8, 3072, 4608], P('exp', None, 'ctx'), may hold values from -0.109375 to 0.109375
- expert_down: bfloat16 [8, 4608, 3072], P('exp', 'ctx'), may hold values from -0.09375 to 0.09375
Outputs:
- query_grad: bfloat16 [768, 1024], P('ctx', 'exp')
- key_grad: bfloat16 [768, 1024], P('ctx', 'exp')
- value_grad: bfloat16 [768, 1024], P('ctx', 'exp')
The draws below stay inside these ranges and needn't reach their ends.
Inputs may be any that keep to these rules, and one draw needn't show every extreme that they name: `experts_of`: in each aligned block of 24 tokens (the tokens of one device) no expert is named by more than 9 tokens, a bound that some block reaches; a token's two experts differ.
All inputs are finite; a program needn't handle non-finite values.
Results may differ from the reference program's by a relative error of at most 0.017.
Values may be sent and summed in bfloat16 or wider, within the bound.
A program may use at most 128 MiB of HBM per device.

```python
import math
from functools import partial
import jax
import jax.numpy as jnp
import numpy as np
from jax import lax

D = 3072
F = 4608
HD = 128
TOK_DEV = 24
HEAD_COUNT = 8
EXPERTS = 8
D_ATTN = 1024
F_PART = 1152
CAP = 9
BLOCK = 192
WINDOW_TOKENS = 768
N_CTX = 4
N_EXP = 8


def draw_log_decay(key, part):
    random_subkeys = jax.random.split(key, 6)
    share = 0.5
    rapid_head = jax.random.uniform(random_subkeys[0], (HEAD_COUNT, 1), jnp.float32) < share
    rapid_decay_rate = jnp.exp(jax.random.uniform(random_subkeys[1], (HEAD_COUNT, 1), jnp.float32, math.log(1.0 / 50.0), math.log(1.0 / 30.0)))
    gentle_decay_rate = jnp.exp(jax.random.uniform(random_subkeys[2], (HEAD_COUNT, 1), jnp.float32, math.log(0.05 / WINDOW_TOKENS), math.log(0.6 / WINDOW_TOKENS)))
    random_offset = jax.random.uniform(random_subkeys[3], (HEAD_COUNT, WINDOW_TOKENS), jnp.float32, 0.5, 1.5)
    spike_position = jax.random.randint(random_subkeys[4], (HEAD_COUNT, 2), 0, WINDOW_TOKENS)
    token_position = jnp.arange(WINDOW_TOKENS, dtype=jnp.int32)[None, :]
    spike_flag = (token_position == spike_position[:, 0:1]) | (token_position == spike_position[:, 1:2])
    spike_penalty = jax.random.uniform(random_subkeys[5], (HEAD_COUNT, WINDOW_TOKENS), jnp.float32, math.log(1.25), math.log(2.0))
    per_step_rate = jnp.where(rapid_head, rapid_decay_rate, gentle_decay_rate) * random_offset + jnp.where(spike_flag, spike_penalty, 0.0)
    return (-per_step_rate).astype(jnp.float32)


def draw_residual(key, part):
    random_subkeys = jax.random.split(key, 3)
    base_draw = jnp.clip(jax.random.normal(random_subkeys[0], (WINDOW_TOKENS, D), jnp.float32), -4.0, 4.0)
    row_scale = jnp.exp(jax.random.uniform(random_subkeys[1], (WINDOW_TOKENS, 1), jnp.float32, math.log(0.05), math.log(0.5)))
    col_scale = jnp.exp(jax.random.uniform(random_subkeys[2], (1, D), jnp.float32, 0.0, math.log(10.0)))
    return (base_draw * row_scale * col_scale).astype(jnp.bfloat16)


def shard_levels(stream_key, shape, shards, least, largest):
    factor_of, own = 1.0, jax.random.fold_in(stream_key, 6)
    for axis_at, parts in shards:
        heights = jnp.exp(jax.random.uniform(jax.random.fold_in(own, axis_at), (parts,), jnp.float32, least / len(shards), largest / len(shards)))
        factor_of = factor_of * jnp.repeat(heights, shape[axis_at] // parts).reshape([-1 if axis == axis_at else 1 for axis in range(len(shape))])
    return factor_of


def deal_out(rng, own, number, rows, count, top, limit, skew):
    ranking = jax.random.permutation(rng, count)
    crowded, usual = load_shares(count, rows * top, limit, skew, True), load_shares(count, rows * top, limit, skew, False)
    places = jnp.arange(count)

    def named(sizes, offset_by):
        used = int((sizes > 0).sum())
        fixed = max(1, used // 4)
        moved = fixed + (places - fixed + offset_by * (used - fixed)) % max(1, count - fixed)
        return jnp.zeros((count,), jnp.int32).at[ranking[jnp.where(places < fixed, places, moved)]].set(jnp.asarray(sizes, jnp.int32))

    sizes = jnp.where(number % 4 == 0, named(crowded, number // 4), named(usual, number - number // 4 - 1))
    mixed = jax.random.permutation(jax.random.fold_in(own, 3), count)
    donor, sink = mixed[0:count // 2 * 2:2], mixed[1:count // 2 * 2:2]
    slack = jnp.minimum(sizes[donor] - 1, limit - sizes[sink]) // 2
    slack = jnp.where((donor == ranking[0]) | (sink == ranking[0]) | (sizes[sink] == 0), 0, jnp.maximum(slack, 0))
    moved = jax.random.randint(jax.random.fold_in(own, 4), (count // 2,), 0, 1 << 20) % (slack + 1)
    sizes = sizes.at[donor].add(-moved).at[sink].add(moved)
    labels = jnp.searchsorted(jnp.cumsum(sizes), jnp.arange(rows * top), side="right").astype(jnp.int32)
    listing = labels.reshape(top, rows).T
    listing = listing[jax.random.permutation(jax.random.fold_in(own, 1), rows)]
    offset_by = jax.random.randint(jax.random.fold_in(own, 2), (rows, 1), 0, top)
    return jnp.take_along_axis(listing, (jnp.arange(top)[None, :] + offset_by) % top, axis=1)


def load_shares(amount, total, bound, skew, full):
    portions = [(1 << 20) // math.isqrt(rank ** skew) + 1 for rank in range(1, amount + 1)]
    largest = bound if full else min(bound, max(-(-total // amount), total * portions[0] // sum(portions)))
    least = 1 if total - largest >= amount - 1 else 0
    holding, spare = [largest] + [least] * (amount - 1), total - largest - least * (amount - 1)
    while spare > 0:
        movable = [i for i in range(1, amount) if holding[i] < largest] or [i for i in range(1, amount) if holding[i] < bound]
        whole, budget = sum([portions[i] for i in movable]), spare
        for i in movable:
            more = min(bound - holding[i], max(1, budget * portions[i] // whole), spare)
            holding[i] = holding[i] + more
            spare = spare - more
    return np.array(holding)


def normal_values(stream_key, dims, scale, reach, shards=(), kind=jnp.bfloat16):
    loudness = shard_levels(stream_key, dims, shards, -0.22, 0.18) if shards else 1.0
    entries = jax.random.normal(stream_key, dims, jnp.float32) * scale * loudness
    return jnp.minimum(jnp.maximum(entries, -reach), reach).astype(kind)


def setup_inputs(seed: int = 0) -> dict:
    splits = jax.random.split(jax.random.key(seed), 14)
    query_rows = normal_values(splits[0], (WINDOW_TOKENS, D_ATTN), 1.0, 6.0, ((0, 4), (1, 8)))
    key_rows = normal_values(splits[1], (WINDOW_TOKENS, D_ATTN), 1.0, 6.0, ((0, 4), (1, 8)))
    value_rows = normal_values(splits[2], (WINDOW_TOKENS, D_ATTN), 1.0, 6.0, ((0, 4), (1, 8)))
    log_decay = draw_log_decay(jax.random.fold_in(splits[13], 71), 0)
    residual = draw_residual(jax.random.fold_in(splits[13], 71), 0)
    norm_gain = jnp.clip(1.0 + 0.18 * jax.random.normal(splits[5], (D,), jnp.float32), 0.1, 1.9)
    out_grad = normal_values(splits[6], (WINDOW_TOKENS, D), 1.0, 6.0, ((0, 32),))
    experts_of_keys = jax.random.split(jax.random.fold_in(splits[7], 1), WINDOW_TOKENS // TOK_DEV)
    experts_of_turns = jax.random.permutation(jax.random.fold_in(splits[7], 3), WINDOW_TOKENS // TOK_DEV)
    experts_of = jax.vmap(lambda own, number: deal_out(jax.random.fold_in(splits[7], 2), own, number, TOK_DEV, EXPERTS, 2, CAP, 2))(experts_of_keys, experts_of_turns).reshape((WINDOW_TOKENS, 2))
    route_weight = jnp.clip(0.1 + 0.79999997 * jax.random.uniform(splits[8], (WINDOW_TOKENS, 2), jnp.float32) ** shard_levels(splits[8], (WINDOW_TOKENS, 2), ((0, 32),), -0.2, 0.2), 0.1, 0.9)
    output_weight = normal_values(splits[9], (D_ATTN, D), D_ATTN ** -0.5, 0.1875, ((0, 8),))
    expert_gate = normal_values(splits[10], (EXPERTS, D, F), D ** -0.5, 0.109375, ((0, 8), (2, 4)))
    expert_up = normal_values(splits[11], (EXPERTS, D, F), D ** -0.5, 0.109375, ((0, 8), (2, 4)))
    expert_down = normal_values(splits[12], (EXPERTS, F, D), F ** -0.5, 0.09375, ((0, 8), (1, 4)))
    return dict(query_rows=query_rows, key_rows=key_rows, value_rows=value_rows, log_decay=log_decay, residual=residual, norm_gain=norm_gain, out_grad=out_grad, experts_of=experts_of, route_weight=route_weight, output_weight=output_weight, expert_gate=expert_gate, expert_up=expert_up, expert_down=expert_down)


def normalize(residual, norm_gain):
    residual_f = residual.astype(jnp.float32)
    factor = lax.rsqrt(lax.optimization_barrier(jnp.mean(residual_f * residual_f, axis=-1, keepdims=True)) + 1e-05)
    return (residual_f, factor, (residual_f * factor * norm_gain).astype(jnp.bfloat16))

def slot_table(experts_of, count, capacity):
    flat_ids = experts_of.reshape(-1)
    matches = (flat_ids[:, None] == jnp.arange(count, dtype=jnp.int32)[None, :]).astype(jnp.int32)
    before = jnp.cumsum(matches, axis=0, dtype=jnp.int32) - matches
    target = flat_ids * capacity + lax.optimization_barrier(jnp.sum(before * matches, axis=1, dtype=jnp.int32))
    slots = jnp.arange(count * capacity, dtype=jnp.int32)
    return (slots[:, None] == target[None, :]).astype(jnp.bfloat16)

def pack_rows(expert_input, out_grad, route_weight, slot_onehot, count, capacity):
    routed = (route_weight[:, :, None] * out_grad.astype(jnp.float32)[:, None, :]).astype(jnp.bfloat16)
    inputs = jnp.broadcast_to(expert_input[:, None, :], routed.shape)
    packed = jnp.concatenate([inputs, routed], axis=-1).reshape(slot_onehot.shape[1], -1)
    outgoing = jnp.dot(slot_onehot, packed, preferred_element_type=jnp.float32).astype(jnp.bfloat16)
    return outgoing.reshape(count, capacity, packed.shape[1])

def expert_rows(row_block, gate_mat, up_mat, down_mat):
    features = gate_mat.shape[0]
    row_input = row_block[:, :features]
    row_grad = row_block[:, features:]
    gate_pre = jnp.dot(row_input, gate_mat, preferred_element_type=jnp.float32)
    up_pre = jnp.dot(row_input, up_mat, preferred_element_type=jnp.float32)
    hidden_grad = lax.dot_general(row_grad, down_mat, (((1,), (1,)), ((), ())), preferred_element_type=jnp.float32)
    gate_sig = jax.nn.sigmoid(gate_pre)
    gate_grad = (hidden_grad * up_pre * gate_sig * (1.0 + gate_pre * (1.0 - gate_sig))).astype(jnp.bfloat16)
    up_grad = (hidden_grad * gate_pre * gate_sig).astype(jnp.bfloat16)
    first = lax.dot_general(gate_grad, gate_mat, (((1,), (1,)), ((), ())), preferred_element_type=jnp.float32)
    second = lax.dot_general(up_grad, up_mat, (((1,), (1,)), ((), ())), preferred_element_type=jnp.float32)
    return first + second

def resid_backward(residual_f, factor, out_grad, slot_onehot, returned, norm_gain):
    per_row = lax.dot_general(slot_onehot, returned.reshape(slot_onehot.shape[0], -1), (((0,), (0,)), ((), ())), preferred_element_type=jnp.float32)
    moe_grad = lax.optimization_barrier(jnp.sum(per_row.reshape(-1, 2, per_row.shape[1]), axis=1))
    scaled = norm_gain * moe_grad
    unit_rows = residual_f * factor
    total_grad = out_grad.astype(jnp.float32) + factor * (scaled - unit_rows * lax.optimization_barrier(jnp.mean(unit_rows * scaled, axis=-1, keepdims=True)))
    return total_grad.astype(jnp.bfloat16)

def block_terms(query_part, key_part, value_part, grad_part, log_steps, score_scale):
    levels = jnp.cumsum(log_steps)
    block_total = levels[-1]
    from_start = jnp.exp(levels)
    to_end = jnp.exp(block_total - levels)
    key_state = lax.dot_general(key_part.astype(jnp.float32) * to_end[:, None], value_part.astype(jnp.float32), (((0,), (0,)), ((), ())), precision=lax.Precision.HIGHEST)
    adjoint = score_scale * lax.dot_general(query_part.astype(jnp.float32) * from_start[:, None], grad_part.astype(jnp.float32), (((0,), (0,)), ((), ())), precision=lax.Precision.HIGHEST)
    return (levels, jnp.exp(block_total), key_state, adjoint)

def block_grads(query_part, key_part, value_part, grad_part, levels, state_in, adjoint_out, score_scale):
    block_total = levels[-1]
    from_start = jnp.exp(levels)
    to_end = jnp.exp(block_total - levels)
    token_position = jnp.arange(levels.shape[0], dtype=jnp.int32)
    causal = token_position[:, None] >= token_position[None, :]
    fading = jnp.exp(jnp.where(causal, levels[:, None] - levels[None, :], -jnp.inf))
    scores = lax.dot_general(query_part, key_part, (((1,), (1,)), ((), ())), preferred_element_type=jnp.float32)
    attn_probs = (score_scale * scores * fading).astype(jnp.bfloat16)
    grad_scores = lax.dot_general(grad_part, value_part, (((1,), (1,)), ((), ())), preferred_element_type=jnp.float32)
    pull_weights = (score_scale * grad_scores * fading).astype(jnp.bfloat16)
    grad_f = grad_part.astype(jnp.float32)
    query_out = jnp.dot(pull_weights, key_part, preferred_element_type=jnp.float32)
    query_out = query_out + score_scale * from_start[:, None] * lax.dot_general(grad_f, state_in, (((1,), (1,)), ((), ())), precision=lax.Precision.HIGHEST)
    key_out = lax.dot_general(pull_weights, query_part, (((0,), (0,)), ((), ())), preferred_element_type=jnp.float32)
    key_out = key_out + to_end[:, None] * lax.dot_general(value_part.astype(jnp.float32), adjoint_out, (((1,), (1,)), ((), ())), precision=lax.Precision.HIGHEST)
    value_out = lax.dot_general(attn_probs, grad_part, (((0,), (0,)), ((), ())), preferred_element_type=jnp.float32)
    value_out = value_out + to_end[:, None] * jnp.dot(key_part.astype(jnp.float32), adjoint_out, precision=lax.Precision.HIGHEST)
    return (query_out.astype(jnp.bfloat16), key_out.astype(jnp.bfloat16), value_out.astype(jnp.bfloat16))

def reference(query_rows, key_rows, value_rows, log_decay, residual, norm_gain, out_grad, experts_of, route_weight, output_weight, expert_gate, expert_up, expert_down):
    blocks = N_CTX * N_EXP
    resid_blocks = residual.reshape(blocks, TOK_DEV, D)
    grad_blocks = out_grad.reshape(blocks, TOK_DEV, D)
    route_blocks = experts_of.reshape(blocks, TOK_DEV, 2)
    weight_blocks = route_weight.reshape(blocks, TOK_DEV, 2)
    residual_f, factor, expert_input = jax.vmap(partial(normalize, norm_gain=norm_gain))(resid_blocks)
    dispatches = jax.vmap(partial(slot_table, count=EXPERTS, capacity=CAP))(route_blocks)
    outgoing = jax.vmap(partial(pack_rows, count=EXPERTS, capacity=CAP))(expert_input, grad_blocks, weight_blocks, dispatches)
    by_expert = jnp.transpose(outgoing, (1, 0, 2, 3)).reshape(EXPERTS, blocks * CAP, 2 * D)

    def expert_block(operands):
        row_block, gate_mat, up_mat, down_mat = operands
        summed_rows = jnp.zeros((row_block.shape[0], D), jnp.float32)
        for group_index in range(N_CTX):
            start_unit = group_index * F_PART
            end_unit = start_unit + F_PART
            group_term = expert_rows(row_block, gate_mat[:, start_unit:end_unit], up_mat[:, start_unit:end_unit], down_mat[start_unit:end_unit]).astype(jnp.bfloat16)
            summed_rows = summed_rows + lax.optimization_barrier(group_term).astype(jnp.float32)
        return summed_rows.astype(jnp.bfloat16)
    finished = lax.map(expert_block, (by_expert, expert_gate, expert_up, expert_down))
    returned = jnp.transpose(finished.reshape(EXPERTS, blocks, CAP, D), (1, 0, 2, 3))
    resid_grad = jax.vmap(partial(resid_backward, norm_gain=norm_gain))(residual_f, factor, grad_blocks, dispatches, returned)
    resid_grad = resid_grad.reshape(WINDOW_TOKENS, D)
    attn_grad = lax.dot_general(resid_grad, output_weight, (((1,), (1,)), ((), ())), preferred_element_type=jnp.float32).astype(jnp.bfloat16)
    score_scale = 1.0 / math.sqrt(HD * WINDOW_TOKENS)

    def by_head(array):
        return jnp.transpose(array.reshape(N_CTX, BLOCK, HEAD_COUNT, HD), (2, 0, 1, 3))
    steps_all = log_decay.reshape(HEAD_COUNT, N_CTX, BLOCK)

    def head_backward(operands):
        query_part, key_part, value_part, grad_part, log_steps = operands
        levels, block_gain, key_state, adjoint = jax.vmap(partial(block_terms, score_scale=score_scale))(query_part, key_part, value_part, grad_part, log_steps)
        zero_state = jnp.zeros((HD, HD), jnp.float32)

        def forward_step(carry, element):
            gain_now, state_now = element
            return (gain_now * carry + state_now, carry)
        _, state_in = lax.scan(forward_step, zero_state, (block_gain, key_state))

        def backward_step(carry, element):
            gain_now, adjoint_now = element
            return (adjoint_now + gain_now * carry, carry)
        _, adjoint_out = lax.scan(backward_step, zero_state, (block_gain, adjoint), reverse=True)
        return jax.vmap(partial(block_grads, score_scale=score_scale))(query_part, key_part, value_part, grad_part, levels, state_in, adjoint_out)
    results = lax.map(head_backward, (by_head(query_rows), by_head(key_rows), by_head(value_rows), by_head(attn_grad), steps_all))

    def merge_heads(array):
        return jnp.transpose(array, (1, 2, 0, 3)).reshape(WINDOW_TOKENS, D_ATTN)
    return (merge_heads(results[0]), merge_heads(results[1]), merge_heads(results[2]))
```

```python
import functools
import math

import jax
import jax.numpy as jnp
from jax import lax
from jax.experimental import pallas as pl
from jax.experimental.pallas import tpu as pltpu
from jax.sharding import PartitionSpec as P

MESH = pl.DeviceIdType.MESH


def exchange_kernel(axis, n, kinds, *refs):
    k = len(kinds)
    ins, outs = refs[:k], refs[k : 2 * k]
    local_sem, send_sem, recv_sem = refs[2 * k :]
    me = lax.axis_index(axis)
    barrier = pltpu.get_barrier_semaphore()
    for s in range(1, n):
        pl.semaphore_signal(
            barrier, inc=1, device_id={axis: lax.rem(me + s, n)}, device_id_type=MESH
        )
    pl.semaphore_wait(barrier, n - 1)

    def source(i, place):
        return ins[i] if kinds[i] == "gather" else ins[i].at[place]

    def remote(i, s, place):
        peer = lax.rem(me + s, n)
        return pltpu.make_async_remote_copy(
            src_ref=source(i, peer),
            dst_ref=outs[i].at[place],
            send_sem=send_sem.at[i, s - 1],
            recv_sem=recv_sem.at[i, s - 1],
            device_id={axis: peer},
            device_id_type=MESH,
        )

    sent = [remote(i, s, me) for i in range(k) for s in range(1, n)]
    for copy in sent:
        copy.start()
    own = [
        pltpu.make_async_copy(source(i, me), outs[i].at[me], local_sem.at[i]) for i in range(k)
    ]
    for copy in own:
        copy.start()
    for copy in own:
        copy.wait()
    for i in range(k):
        for s in range(1, n):
            remote(i, s, lax.rem(me - s + n, n)).wait_recv()
    for copy in sent:
        copy.wait_send()


def exchange(axis, collective_id, arrays, kinds):
    n = lax.axis_size(axis)
    k = len(arrays)
    shapes = [
        jax.ShapeDtypeStruct((n,) + a.shape if kind == "gather" else a.shape, a.dtype)
        for a, kind in zip(arrays, kinds)
    ]
    return pl.pallas_call(
        functools.partial(exchange_kernel, axis, n, kinds),
        out_shape=shapes,
        in_specs=[pl.BlockSpec(memory_space=pl.ANY)] * k,
        out_specs=[pl.BlockSpec(memory_space=pl.ANY)] * k,
        scratch_shapes=[
            pltpu.SemaphoreType.DMA((k,)),
            pltpu.SemaphoreType.DMA((k, n - 1)),
            pltpu.SemaphoreType.DMA((k, n - 1)),
        ],
        compiler_params=pltpu.CompilerParams(collective_id=collective_id, has_side_effects=True),
    )(*arrays)


def dot_bt(a, b):
    return lax.dot_general(a, b, (((1,), (1,)), ((), ())), preferred_element_type=jnp.float32)


def expert_kernel(x_ref, g_ref, gate_ref, up_ref, down_ref, out_ref, acc_ref):
    step = pl.program_id(0)
    gate_mat = gate_ref[0]
    up_mat = up_ref[0]
    gate_pre = jnp.dot(x_ref[...], gate_mat, preferred_element_type=jnp.float32)
    up_pre = jnp.dot(x_ref[...], up_mat, preferred_element_type=jnp.float32)
    hidden_grad = dot_bt(g_ref[...], down_ref[0])
    gate_sig = 1.0 / (1.0 + jnp.exp(-gate_pre))
    gate_grad = (hidden_grad * up_pre * gate_sig * (1.0 + gate_pre * (1.0 - gate_sig))).astype(
        jnp.bfloat16
    )
    up_grad = (hidden_grad * gate_pre * gate_sig).astype(jnp.bfloat16)
    term = dot_bt(gate_grad, gate_mat) + dot_bt(up_grad, up_mat)

    @pl.when(step == 0)
    def _():
        acc_ref[...] = term

    @pl.when(step > 0)
    def _():
        acc_ref[...] += term

    @pl.when(step == pl.num_programs(0) - 1)
    def _():
        count, _, half = out_ref.shape
        rows = acc_ref.shape[0] // count
        for d in range(count):
            part = acc_ref[d * rows : (d + 1) * rows, :]
            out_ref[d] = jnp.concatenate([part[:, :half], part[:, half:]], axis=0).astype(
                jnp.bfloat16
            )


def expert_rows(x, g, gate, up, down, count):
    rows, features = x.shape
    hidden = gate.shape[2]
    tile = next((t for t in (384, 256, 128) if hidden % t == 0), hidden)
    half = features // 2
    return pl.pallas_call(
        expert_kernel,
        grid=(hidden // tile,),
        out_shape=jax.ShapeDtypeStruct((count, 2 * (rows // count), half), jnp.bfloat16),
        in_specs=[
            pl.BlockSpec((rows, features), lambda f: (0, 0)),
            pl.BlockSpec((rows, features), lambda f: (0, 0)),
            pl.BlockSpec((1, features, tile), lambda f: (0, 0, f)),
            pl.BlockSpec((1, features, tile), lambda f: (0, 0, f)),
            pl.BlockSpec((1, tile, features), lambda f: (0, f, 0)),
        ],
        out_specs=pl.BlockSpec((count, 2 * (rows // count), half), lambda f: (0, 0, 0)),
        scratch_shapes=[pltpu.VMEM((rows, features), jnp.float32)],
        compiler_params=pltpu.CompilerParams(vmem_limit_bytes=60 * 2**20),
    )(x, g, gate, up, down)


def normalize(residual, norm_gain):
    residual_f = residual.astype(jnp.float32)
    factor = lax.rsqrt(jnp.mean(residual_f * residual_f, axis=-1, keepdims=True) + 1e-05)
    return (residual_f, factor, (residual_f * factor * norm_gain).astype(jnp.bfloat16))


def block_terms(key_part, value_part, log_steps):
    place = jnp.arange(log_steps.shape[0], dtype=jnp.int32)
    levels = jnp.sum(
        jnp.where(place[:, None] >= place[None, :], log_steps[None, :], 0.0), axis=1
    )
    block_total = levels[-1]
    to_end = jnp.exp(block_total - levels)
    key_state = lax.dot_general(
        key_part.astype(jnp.float32) * to_end[:, None],
        value_part.astype(jnp.float32),
        (((0,), (0,)), ((), ())),
        precision=lax.Precision.HIGHEST,
    )
    return (levels, block_total, key_state)


def block_grads(
    query_part, key_part, value_part, grad_part, levels, state_in, adjoint_out, score_scale
):
    block_total = levels[-1]
    from_start = jnp.exp(levels)
    to_end = jnp.exp(block_total - levels)
    token_position = jnp.arange(levels.shape[0], dtype=jnp.int32)
    causal = token_position[:, None] >= token_position[None, :]
    fading = jnp.exp(jnp.where(causal, levels[:, None] - levels[None, :], -jnp.inf))
    scores = lax.dot_general(
        query_part, key_part, (((1,), (1,)), ((), ())), preferred_element_type=jnp.float32
    )
    attn_probs = (score_scale * scores * fading).astype(jnp.bfloat16)
    grad_scores = lax.dot_general(
        grad_part, value_part, (((1,), (1,)), ((), ())), preferred_element_type=jnp.float32
    )
    pull_weights = (score_scale * grad_scores * fading).astype(jnp.bfloat16)
    grad_f = grad_part.astype(jnp.float32)
    query_out = jnp.dot(pull_weights, key_part, preferred_element_type=jnp.float32)
    query_out = query_out + score_scale * from_start[:, None] * lax.dot_general(
        grad_f, state_in, (((1,), (1,)), ((), ())), precision=lax.Precision.HIGHEST
    )
    key_out = lax.dot_general(
        pull_weights, query_part, (((0,), (0,)), ((), ())), preferred_element_type=jnp.float32
    )
    key_out = key_out + to_end[:, None] * lax.dot_general(
        value_part.astype(jnp.float32),
        adjoint_out,
        (((1,), (1,)), ((), ())),
        precision=lax.Precision.HIGHEST,
    )
    value_out = lax.dot_general(
        attn_probs, grad_part, (((0,), (0,)), ((), ())), preferred_element_type=jnp.float32
    )
    value_out = value_out + to_end[:, None] * jnp.dot(
        key_part.astype(jnp.float32), adjoint_out, precision=lax.Precision.HIGHEST
    )
    return (
        query_out.astype(jnp.bfloat16),
        key_out.astype(jnp.bfloat16),
        value_out.astype(jnp.bfloat16),
    )


def body(
    query_rows,
    key_rows,
    value_rows,
    log_decay,
    residual,
    norm_gain,
    out_grad,
    experts_of,
    route_weight,
    output_weight,
    expert_gate,
    expert_up,
    expert_down,
):
    ctx_count = lax.axis_size("ctx")
    exp_count = lax.axis_size("exp")
    ctx_place = lax.axis_index("ctx")
    token_count = residual.shape[0]
    features = residual.shape[1]
    half = features // 2
    capacity = max(2, 3 * token_count // exp_count)
    depth = -(-ctx_count * capacity // 8) * 8
    slots = exp_count * depth
    all_tokens = ctx_count * token_count

    residual_f, factor, expert_input = normalize(residual, norm_gain)
    levels, block_total, key_state = block_terms(key_rows, value_rows, log_decay[0])
    meta = jnp.concatenate(
        [
            experts_of.T.astype(jnp.float32),
            route_weight.T,
            jnp.broadcast_to(block_total, (1, token_count)),
        ],
        axis=0,
    )
    meta = jnp.pad(meta, ((0, 3), (0, 128 - token_count)))
    tokens, metas, key_states = exchange(
        "ctx",
        0,
        [jnp.concatenate([expert_input, out_grad], axis=0), meta, key_state],
        ("gather", "gather", "gather"),
    )

    choice = metas[:, 0:2, :token_count].astype(jnp.int32)
    choice_by_token = jnp.transpose(choice, (0, 2, 1)).reshape(-1)
    weights = jnp.transpose(metas[:, 2:4, :token_count], (0, 2, 1)).reshape(-1)
    order = jnp.arange(2 * all_tokens, dtype=jnp.int32)
    ahead = (choice_by_token[:, None] == choice_by_token[None, :]) & (
        order[:, None] > order[None, :]
    )
    target = choice_by_token * depth + jnp.sum(ahead, axis=1, dtype=jnp.int32)
    slot_ids = jnp.arange(slots, dtype=jnp.int32)
    hits = (slot_ids[:, None] == target[None, :]).astype(jnp.float32)
    slot_weight = jnp.sum(hits * weights[None, :], axis=1)
    pick = jnp.sum(hits.reshape(exp_count, depth, ctx_count, token_count, 2), axis=-1)
    none = jnp.zeros_like(pick)
    pick_both = jnp.concatenate(
        [
            jnp.concatenate([pick, none], axis=3),
            jnp.concatenate([none, pick], axis=3),
        ],
        axis=1,
    ).reshape(2 * slots, 2 * all_tokens)
    row_scale = jnp.concatenate(
        [jnp.ones((exp_count, depth), jnp.float32), slot_weight.reshape(exp_count, depth)], axis=1
    )
    outgoing = jnp.dot(
        pick_both.astype(jnp.bfloat16),
        tokens.reshape(2 * all_tokens, features),
        preferred_element_type=jnp.float32,
    )
    outgoing = (outgoing * row_scale.reshape(-1, 1)).astype(jnp.bfloat16)
    [arrived] = exchange(
        "exp", 1, [outgoing.reshape(exp_count, 2 * depth, features)], ("swap",)
    )
    partials = expert_rows(
        arrived[:, :depth].reshape(slots, features),
        arrived[:, depth:].reshape(slots, features),
        expert_gate,
        expert_up,
        expert_down,
        exp_count,
    )
    [returned] = exchange("exp", 2, [partials], ("swap",))

    back = jnp.transpose(pick, (2, 3, 0, 1))[:, None, :, :, None, :]
    halves = jnp.eye(2, dtype=jnp.float32)[None, :, None, None, :, None]
    merge = (back * halves).reshape(2 * all_tokens, 2 * slots).astype(jnp.bfloat16)
    sums = jnp.dot(
        merge, returned.reshape(2 * slots, half), preferred_element_type=jnp.float32
    ).astype(jnp.bfloat16)
    [groups] = exchange(
        "ctx", 3, [sums.reshape(ctx_count, 2 * token_count, half)], ("swap",)
    )

    def split(a):
        return jnp.stack([a[:, :half], a[:, half:]], axis=0)

    moe_grad = jnp.sum(groups.astype(jnp.float32), axis=0).reshape(2, token_count, half)
    scaled = norm_gain.reshape(2, 1, half) * moe_grad
    unit_rows = split(residual_f * factor)
    mean = jnp.sum(unit_rows * scaled, axis=(0, 2), keepdims=True) * (1.0 / features)
    total_grad = split(out_grad.astype(jnp.float32)) + factor[None] * (scaled - unit_rows * mean)
    resid_grad = total_grad.astype(jnp.bfloat16).reshape(2 * token_count, half)
    [resid_all] = exchange("exp", 4, [resid_grad], ("gather",))
    resid_all = resid_all.reshape(exp_count, 2, token_count, half)
    block_len = query_rows.shape[0]
    head_size = query_rows.shape[1]
    attn_grad = (
        dot_bt(resid_all[:, 0].reshape(block_len, half), output_weight[:, :half])
        + dot_bt(resid_all[:, 1].reshape(block_len, half), output_weight[:, half:])
    ).astype(jnp.bfloat16)
    score_scale = 1.0 / math.sqrt(head_size * block_len * ctx_count)
    adjoint = score_scale * lax.dot_general(
        query_rows.astype(jnp.float32) * jnp.exp(levels)[:, None],
        attn_grad.astype(jnp.float32),
        (((0,), (0,)), ((), ())),
        precision=lax.Precision.HIGHEST,
    )
    [adjoints] = exchange("ctx", 5, [adjoint], ("gather",))

    totals = metas[:, 4, 0]
    place = jnp.arange(ctx_count, dtype=jnp.int32)
    between = (place[None, :] > jnp.minimum(place, ctx_place)[:, None]) & (
        place[None, :] < jnp.maximum(place, ctx_place)[:, None]
    )
    decay = jnp.exp(jnp.sum(jnp.where(between, totals[None, :], 0.0), axis=1))
    before = jnp.where(place < ctx_place, decay, 0.0)
    after = jnp.where(place > ctx_place, decay, 0.0)
    state_in = jnp.sum(before[:, None, None] * key_states, axis=0)
    adjoint_out = jnp.sum(after[:, None, None] * adjoints, axis=0)
    return block_grads(
        query_rows, key_rows, value_rows, attn_grad, levels, state_in, adjoint_out, score_scale
    )


def solution(mesh):
    placed = (
        P("ctx", "exp"),
        P("ctx", "exp"),
        P("ctx", "exp"),
        P("exp", "ctx"),
        P(("ctx", "exp"), None),
        P(),
        P(("ctx", "exp"), None),
        P(("ctx", "exp"), None),
        P(("ctx", "exp"), None),
        P("exp", None),
        P("exp", None, "ctx"),
        P("exp", None, "ctx"),
        P("exp", "ctx", None),
    )
    return jax.shard_map(
        body,
        mesh=mesh,
        in_specs=placed,
        out_specs=(P("ctx", "exp"), P("ctx", "exp"), P("ctx", "exp")),
        check_vma=False,
    )
```

```python
import functools
import math

import jax
import jax.numpy as jnp
from jax import lax
from jax.experimental import pallas as pl
from jax.experimental.pallas import tpu as pltpu
from jax.sharding import PartitionSpec as P

MESH = pl.DeviceIdType.MESH


def exchange_kernel(axis, n, kinds, *refs):
    k = len(kinds)
    ins, outs = refs[:k], refs[k : 2 * k]
    local_sem, send_sem, recv_sem = refs[2 * k :]
    me = lax.axis_index(axis)
    barrier = pltpu.get_barrier_semaphore()
    for s in range(1, n):
        pl.semaphore_signal(
            barrier, inc=1, device_id={axis: lax.rem(me + s, n)}, device_id_type=MESH
        )
    pl.semaphore_wait(barrier, n - 1)

    def source(i, place):
        return ins[i] if kinds[i] == "gather" else ins[i].at[place]

    def remote(i, s, place):
        peer = lax.rem(me + s, n)
        return pltpu.make_async_remote_copy(
            src_ref=source(i, peer),
            dst_ref=outs[i].at[place],
            send_sem=send_sem.at[i, s - 1],
            recv_sem=recv_sem.at[i, s - 1],
            device_id={axis: peer},
            device_id_type=MESH,
        )

    sent = [remote(i, s, me) for i in range(k) for s in range(1, n)]
    for copy in sent:
        copy.start()
    own = [
        pltpu.make_async_copy(source(i, me), outs[i].at[me], local_sem.at[i]) for i in range(k)
    ]
    for copy in own:
        copy.start()
    for copy in own:
        copy.wait()
    for i in range(k):
        for s in range(1, n):
            remote(i, s, lax.rem(me - s + n, n)).wait_recv()
    for copy in sent:
        copy.wait_send()


def exchange(axis, collective_id, arrays, kinds):
    n = lax.axis_size(axis)
    k = len(arrays)
    shapes = [
        jax.ShapeDtypeStruct((n,) + a.shape if kind == "gather" else a.shape, a.dtype)
        for a, kind in zip(arrays, kinds)
    ]
    return pl.pallas_call(
        functools.partial(exchange_kernel, axis, n, kinds),
        out_shape=shapes,
        in_specs=[pl.BlockSpec(memory_space=pl.ANY)] * k,
        out_specs=[pl.BlockSpec(memory_space=pl.ANY)] * k,
        scratch_shapes=[
            pltpu.SemaphoreType.DMA((k,)),
            pltpu.SemaphoreType.DMA((k, n - 1)),
            pltpu.SemaphoreType.DMA((k, n - 1)),
        ],
        compiler_params=pltpu.CompilerParams(collective_id=collective_id, has_side_effects=True),
    )(*arrays)


def relay_kernel(axes, counts, kind, width, src, mat, scale, out, got, made, *sems):
    local_sem, first_send, first_recv, second_send, second_recv, own_sem = sems
    chunks = src.shape[-1] // width
    me = [lax.axis_index(axis) for axis in axes]
    barrier = pltpu.get_barrier_semaphore()
    for axis, place, n in zip(axes, me, counts):
        for s in range(1, n):
            pl.semaphore_signal(
                barrier, inc=1, device_id={axis: lax.rem(place + s, n)}, device_id_type=MESH
            )
    pl.semaphore_wait(barrier, counts[0] + counts[1] - 2)

    def columns(c):
        return pl.ds(c * width, width)

    def part(c, place):
        return src.at[:, columns(c)] if kind == "gather" else src.at[place, :, columns(c)]

    def first(c, s, place):
        peer = lax.rem(me[0] + s, counts[0])
        return pltpu.make_async_remote_copy(
            src_ref=part(c, peer),
            dst_ref=got.at[place, :, columns(c)],
            send_sem=first_send.at[c, s - 1],
            recv_sem=first_recv.at[c, s - 1],
            device_id={axes[0]: peer},
            device_id_type=MESH,
        )

    def second(c, s, place):
        peer = lax.rem(me[1] + s, counts[1])
        return pltpu.make_async_remote_copy(
            src_ref=made.at[peer, :, columns(c)],
            dst_ref=out.at[place, :, columns(c)],
            send_sem=second_send.at[c, s - 1],
            recv_sem=second_recv.at[c, s - 1],
            device_id={axes[1]: peer},
            device_id_type=MESH,
        )

    sent = []
    kept = []
    for c in range(chunks):
        for s in range(1, counts[0]):
            copy = first(c, s, me[0])
            copy.start()
            sent.append(copy)
        copy = pltpu.make_async_copy(
            part(c, me[0]), got.at[me[0], :, columns(c)], local_sem.at[c]
        )
        copy.start()
        kept.append(copy)
    for c in range(chunks):
        kept[c].wait()
        for s in range(1, counts[0]):
            first(c, s, lax.rem(me[0] - s + counts[0], counts[0])).wait_recv()
        rows = got[:, :, columns(c)].reshape(-1, width)
        term = jnp.dot(mat[...], rows, preferred_element_type=jnp.float32)
        term = (term * scale[...]).astype(jnp.bfloat16)
        made[:, :, columns(c)] = term.reshape(made.shape[0], made.shape[1], width)
        for s in range(1, counts[1]):
            copy = second(c, s, me[1])
            copy.start()
            sent.append(copy)
        copy = pltpu.make_async_copy(
            made.at[me[1], :, columns(c)], out.at[me[1], :, columns(c)], own_sem.at[c]
        )
        copy.start()
        kept.append(copy)
    for c in range(chunks):
        kept[chunks + c].wait()
        for s in range(1, counts[1]):
            second(c, s, lax.rem(me[1] - s + counts[1], counts[1])).wait_recv()
    for copy in sent:
        copy.wait_send()


def relay(axes, collective_id, kind, width, src, mat, scale):
    counts = [lax.axis_size(axis) for axis in axes]
    rows, total = src.shape[-2:]
    out_shape = (counts[1], mat.shape[0] // counts[1], total)
    chunks = total // width
    vmem = pl.BlockSpec(memory_space=pltpu.VMEM)
    return pl.pallas_call(
        functools.partial(relay_kernel, axes, counts, kind, width),
        out_shape=jax.ShapeDtypeStruct(out_shape, jnp.bfloat16),
        in_specs=[pl.BlockSpec(memory_space=pl.ANY), vmem, vmem],
        out_specs=pl.BlockSpec(memory_space=pl.ANY),
        scratch_shapes=[
            pltpu.VMEM((counts[0], rows, total), jnp.bfloat16),
            pltpu.VMEM(out_shape, jnp.bfloat16),
            pltpu.SemaphoreType.DMA((chunks,)),
            pltpu.SemaphoreType.DMA((chunks, counts[0] - 1)),
            pltpu.SemaphoreType.DMA((chunks, counts[0] - 1)),
            pltpu.SemaphoreType.DMA((chunks, counts[1] - 1)),
            pltpu.SemaphoreType.DMA((chunks, counts[1] - 1)),
            pltpu.SemaphoreType.DMA((chunks,)),
        ],
        compiler_params=pltpu.CompilerParams(
            collective_id=collective_id, has_side_effects=True, vmem_limit_bytes=40 * 2**20
        ),
    )(src, mat, scale)


def dot_bt(a, b):
    return lax.dot_general(a, b, (((1,), (1,)), ((), ())), preferred_element_type=jnp.float32)


def expert_kernel(rows_ref, gate_ref, up_ref, down_ref, out_ref, x_ref, g_ref, acc_ref):
    step = pl.program_id(0)

    @pl.when(step == 0)
    def _():
        pair = rows_ref.shape[1]
        depth = pair // 2
        for p in range(rows_ref.shape[0] // 2):
            one = rows_ref[2 * p].astype(jnp.float32)
            two = rows_ref[2 * p + 1].astype(jnp.float32)
            for ref, cut in ((x_ref, slice(0, depth)), (g_ref, slice(depth, pair))):
                ref[p * pair : (p + 1) * pair, :] = jnp.concatenate(
                    [one[cut], two[cut]], axis=0
                ).astype(jnp.bfloat16)

    gate_mat = gate_ref[0]
    up_mat = up_ref[0]
    gate_pre = jnp.dot(x_ref[...], gate_mat, preferred_element_type=jnp.float32)
    up_pre = jnp.dot(x_ref[...], up_mat, preferred_element_type=jnp.float32)
    hidden_grad = dot_bt(g_ref[...], down_ref[0])
    gate_sig = 1.0 / (1.0 + jnp.exp(-gate_pre))
    gate_grad = (hidden_grad * up_pre * gate_sig * (1.0 + gate_pre * (1.0 - gate_sig))).astype(
        jnp.bfloat16
    )
    up_grad = (hidden_grad * gate_pre * gate_sig).astype(jnp.bfloat16)
    term = dot_bt(gate_grad, gate_mat) + dot_bt(up_grad, up_mat)

    @pl.when(step == 0)
    def _():
        acc_ref[...] = term

    @pl.when(step > 0)
    def _():
        acc_ref[...] += term

    @pl.when(step == pl.num_programs(0) - 1)
    def _():
        count, _, half = out_ref.shape
        rows = acc_ref.shape[0] // count
        for d in range(count):
            part = acc_ref[d * rows : (d + 1) * rows, :]
            out_ref[d] = jnp.concatenate([part[:, :half], part[:, half:]], axis=0).astype(
                jnp.bfloat16
            )


def expert_rows(arrived, gate, up, down):
    count, depth, features = arrived.shape
    rows = count * depth // 2
    hidden = gate.shape[2]
    tile = next((t for t in (384, 256, 128) if hidden % t == 0), hidden)
    out_shape = (count, depth, features // 2)
    return pl.pallas_call(
        expert_kernel,
        grid=(hidden // tile,),
        out_shape=jax.ShapeDtypeStruct(out_shape, jnp.bfloat16),
        in_specs=[
            pl.BlockSpec(arrived.shape, lambda f: (0, 0, 0)),
            pl.BlockSpec((1, features, tile), lambda f: (0, 0, f)),
            pl.BlockSpec((1, features, tile), lambda f: (0, 0, f)),
            pl.BlockSpec((1, tile, features), lambda f: (0, f, 0)),
        ],
        out_specs=pl.BlockSpec(out_shape, lambda f: (0, 0, 0)),
        scratch_shapes=[
            pltpu.VMEM((rows, features), jnp.bfloat16),
            pltpu.VMEM((rows, features), jnp.bfloat16),
            pltpu.VMEM((rows, features), jnp.float32),
        ],
        compiler_params=pltpu.CompilerParams(vmem_limit_bytes=60 * 2**20),
    )(arrived, gate, up, down)


def normalize(residual, norm_gain):
    residual_f = residual.astype(jnp.float32)
    factor = lax.rsqrt(jnp.mean(residual_f * residual_f, axis=-1, keepdims=True) + 1e-05)
    return (residual_f, factor, (residual_f * factor * norm_gain).astype(jnp.bfloat16))


def block_terms(key_part, value_part, log_steps):
    place = jnp.arange(log_steps.shape[0], dtype=jnp.int32)
    levels = jnp.sum(
        jnp.where(place[:, None] >= place[None, :], log_steps[None, :], 0.0), axis=1
    )
    block_total = levels[-1]
    to_end = jnp.exp(block_total - levels)
    key_state = lax.dot_general(
        key_part.astype(jnp.float32) * to_end[:, None],
        value_part.astype(jnp.float32),
        (((0,), (0,)), ((), ())),
        precision=lax.Precision.HIGHEST,
    )
    return (levels, block_total, key_state)


def block_grads(
    query_part, key_part, value_part, grad_part, levels, state_in, adjoint_out, score_scale
):
    block_total = levels[-1]
    from_start = jnp.exp(levels)
    to_end = jnp.exp(block_total - levels)
    token_position = jnp.arange(levels.shape[0], dtype=jnp.int32)
    causal = token_position[:, None] >= token_position[None, :]
    fading = jnp.exp(jnp.where(causal, levels[:, None] - levels[None, :], -jnp.inf))
    scores = lax.dot_general(
        query_part, key_part, (((1,), (1,)), ((), ())), preferred_element_type=jnp.float32
    )
    attn_probs = (score_scale * scores * fading).astype(jnp.bfloat16)
    grad_scores = lax.dot_general(
        grad_part, value_part, (((1,), (1,)), ((), ())), preferred_element_type=jnp.float32
    )
    pull_weights = (score_scale * grad_scores * fading).astype(jnp.bfloat16)
    grad_f = grad_part.astype(jnp.float32)
    query_out = jnp.dot(pull_weights, key_part, preferred_element_type=jnp.float32)
    query_out = query_out + score_scale * from_start[:, None] * lax.dot_general(
        grad_f, state_in, (((1,), (1,)), ((), ())), precision=lax.Precision.HIGHEST
    )
    key_out = lax.dot_general(
        pull_weights, query_part, (((0,), (0,)), ((), ())), preferred_element_type=jnp.float32
    )
    key_out = key_out + to_end[:, None] * lax.dot_general(
        value_part.astype(jnp.float32),
        adjoint_out,
        (((1,), (1,)), ((), ())),
        precision=lax.Precision.HIGHEST,
    )
    value_out = lax.dot_general(
        attn_probs, grad_part, (((0,), (0,)), ((), ())), preferred_element_type=jnp.float32
    )
    value_out = value_out + to_end[:, None] * jnp.dot(
        key_part.astype(jnp.float32), adjoint_out, precision=lax.Precision.HIGHEST
    )
    return (
        query_out.astype(jnp.bfloat16),
        key_out.astype(jnp.bfloat16),
        value_out.astype(jnp.bfloat16),
    )


def body(
    query_rows,
    key_rows,
    value_rows,
    log_decay,
    residual,
    norm_gain,
    out_grad,
    experts_of,
    route_weight,
    output_weight,
    expert_gate,
    expert_up,
    expert_down,
):
    ctx_count = lax.axis_size("ctx")
    exp_count = lax.axis_size("exp")
    ctx_place = lax.axis_index("ctx")
    token_count = residual.shape[0]
    features = residual.shape[1]
    half = features // 2
    capacity = max(2, 3 * token_count // exp_count)
    depth = -(-ctx_count * capacity // 8) * 8
    slots = exp_count * depth
    all_tokens = ctx_count * token_count

    residual_f, factor, expert_input = normalize(residual, norm_gain)
    levels, block_total, key_state = block_terms(key_rows, value_rows, log_decay[0])
    meta = jnp.concatenate(
        [
            experts_of.T.astype(jnp.float32),
            route_weight.T,
            jnp.broadcast_to(block_total, (1, token_count)),
        ],
        axis=0,
    )
    meta = jnp.pad(meta, ((0, 3), (0, 128 - token_count)))
    metas, key_states = exchange("ctx", 0, [meta, key_state], ("gather", "gather"))

    choice = metas[:, 0:2, :token_count].astype(jnp.int32)
    choice_by_token = jnp.transpose(choice, (0, 2, 1)).reshape(-1)
    weights = jnp.transpose(metas[:, 2:4, :token_count], (0, 2, 1)).reshape(-1)
    order = jnp.arange(2 * all_tokens, dtype=jnp.int32)
    ahead = (choice_by_token[:, None] == choice_by_token[None, :]) & (
        order[:, None] > order[None, :]
    )
    target = choice_by_token * depth + jnp.sum(ahead, axis=1, dtype=jnp.int32)
    slot_ids = jnp.arange(slots, dtype=jnp.int32)
    hits = (slot_ids[:, None] == target[None, :]).astype(jnp.float32)
    slot_weight = jnp.sum(hits * weights[None, :], axis=1)
    pick = jnp.sum(hits.reshape(exp_count, depth, ctx_count, token_count, 2), axis=-1)
    none = jnp.zeros_like(pick)
    pick_both = jnp.concatenate(
        [
            jnp.concatenate([pick, none], axis=3),
            jnp.concatenate([none, pick], axis=3),
        ],
        axis=1,
    ).reshape(2 * slots, 2 * all_tokens)
    row_scale = jnp.concatenate(
        [jnp.ones((exp_count, depth), jnp.float32), slot_weight.reshape(exp_count, depth)], axis=1
    )
    arrived = relay(
        ("ctx", "exp"),
        1,
        "gather",
        features // 4,
        jnp.concatenate([expert_input, out_grad], axis=0),
        pick_both.astype(jnp.bfloat16),
        row_scale.reshape(-1, 1),
    )
    partials = expert_rows(arrived, expert_gate, expert_up, expert_down)

    back = jnp.transpose(pick, (2, 3, 0, 1))[:, None, :, :, None, :]
    halves = jnp.eye(2, dtype=jnp.float32)[None, :, None, None, :, None]
    merge = (back * halves).reshape(2 * all_tokens, 2 * slots).astype(jnp.bfloat16)
    groups = relay(
        ("exp", "ctx"),
        2,
        "swap",
        half // 3,
        partials,
        merge,
        jnp.ones((2 * all_tokens, 1), jnp.float32),
    )

    def split(a):
        return jnp.stack([a[:, :half], a[:, half:]], axis=0)

    moe_grad = jnp.sum(groups.astype(jnp.float32), axis=0).reshape(2, token_count, half)
    scaled = norm_gain.reshape(2, 1, half) * moe_grad
    unit_rows = split(residual_f * factor)
    mean = jnp.sum(unit_rows * scaled, axis=(0, 2), keepdims=True) * (1.0 / features)
    total_grad = split(out_grad.astype(jnp.float32)) + factor[None] * (scaled - unit_rows * mean)
    resid_grad = total_grad.astype(jnp.bfloat16).reshape(2 * token_count, half)
    [resid_all] = exchange("exp", 4, [resid_grad], ("gather",))
    resid_all = resid_all.reshape(exp_count, 2, token_count, half)
    block_len = query_rows.shape[0]
    head_size = query_rows.shape[1]
    attn_grad = (
        dot_bt(resid_all[:, 0].reshape(block_len, half), output_weight[:, :half])
        + dot_bt(resid_all[:, 1].reshape(block_len, half), output_weight[:, half:])
    ).astype(jnp.bfloat16)
    score_scale = 1.0 / math.sqrt(head_size * block_len * ctx_count)
    adjoint = score_scale * lax.dot_general(
        query_rows.astype(jnp.float32) * jnp.exp(levels)[:, None],
        attn_grad.astype(jnp.float32),
        (((0,), (0,)), ((), ())),
        precision=lax.Precision.HIGHEST,
    )
    [adjoints] = exchange("ctx", 5, [adjoint], ("gather",))

    totals = metas[:, 4, 0]
    place = jnp.arange(ctx_count, dtype=jnp.int32)
    between = (place[None, :] > jnp.minimum(place, ctx_place)[:, None]) & (
        place[None, :] < jnp.maximum(place, ctx_place)[:, None]
    )
    decay = jnp.exp(jnp.sum(jnp.where(between, totals[None, :], 0.0), axis=1))
    before = jnp.where(place < ctx_place, decay, 0.0)
    after = jnp.where(place > ctx_place, decay, 0.0)
    state_in = jnp.sum(before[:, None, None] * key_states, axis=0)
    adjoint_out = jnp.sum(after[:, None, None] * adjoints, axis=0)
    return block_grads(
        query_rows, key_rows, value_rows, attn_grad, levels, state_in, adjoint_out, score_scale
    )


def solution(mesh):
    placed = (
        P("ctx", "exp"),
        P("ctx", "exp"),
        P("ctx", "exp"),
        P("exp", "ctx"),
        P(("ctx", "exp"), None),
        P(),
        P(("ctx", "exp"), None),
        P(("ctx", "exp"), None),
        P(("ctx", "exp"), None),
        P("exp", None),
        P("exp", None, "ctx"),
        P("exp", None, "ctx"),
        P("exp", "ctx", None),
    )
    return jax.shard_map(
        body,
        mesh=mesh,
        in_specs=placed,
        out_specs=(P("ctx", "exp"), P("ctx", "exp"), P("ctx", "exp")),
        check_vma=False,
    )
```

```python
import functools
import math

import jax
import jax.numpy as jnp
from jax import lax
from jax.experimental import pallas as pl
from jax.experimental.pallas import tpu as pltpu
from jax.sharding import PartitionSpec as P

MESH = pl.DeviceIdType.MESH


def exchange_kernel(axis, n, kinds, *refs):
    k = len(kinds)
    ins, outs = refs[:k], refs[k : 2 * k]
    local_sem, send_sem, recv_sem = refs[2 * k :]
    me = lax.axis_index(axis)
    barrier = pltpu.get_barrier_semaphore()
    for s in range(1, n):
        pl.semaphore_signal(
            barrier, inc=1, device_id={axis: lax.rem(me + s, n)}, device_id_type=MESH
        )
    pl.semaphore_wait(barrier, n - 1)

    def source(i, place):
        return ins[i] if kinds[i] == "gather" else ins[i].at[place]

    def remote(i, s, place):
        peer = lax.rem(me + s, n)
        return pltpu.make_async_remote_copy(
            src_ref=source(i, peer),
            dst_ref=outs[i].at[place],
            send_sem=send_sem.at[i, s - 1],
            recv_sem=recv_sem.at[i, s - 1],
            device_id={axis: peer},
            device_id_type=MESH,
        )

    sent = [remote(i, s, me) for i in range(k) for s in range(1, n)]
    for copy in sent:
        copy.start()
    own = [
        pltpu.make_async_copy(source(i, me), outs[i].at[me], local_sem.at[i]) for i in range(k)
    ]
    for copy in own:
        copy.start()
    for copy in own:
        copy.wait()
    for i in range(k):
        for s in range(1, n):
            remote(i, s, lax.rem(me - s + n, n)).wait_recv()
    for copy in sent:
        copy.wait_send()


def exchange(axis, collective_id, arrays, kinds):
    n = lax.axis_size(axis)
    k = len(arrays)
    shapes = [
        jax.ShapeDtypeStruct((n,) + a.shape if kind == "gather" else a.shape, a.dtype)
        for a, kind in zip(arrays, kinds)
    ]
    return pl.pallas_call(
        functools.partial(exchange_kernel, axis, n, kinds),
        out_shape=shapes,
        in_specs=[pl.BlockSpec(memory_space=pl.ANY)] * k,
        out_specs=[pl.BlockSpec(memory_space=pl.ANY)] * k,
        scratch_shapes=[
            pltpu.SemaphoreType.DMA((k,)),
            pltpu.SemaphoreType.DMA((k, n - 1)),
            pltpu.SemaphoreType.DMA((k, n - 1)),
        ],
        compiler_params=pltpu.CompilerParams(collective_id=collective_id, has_side_effects=True),
    )(*arrays)


def relay_kernel(axes, counts, kind, width, src, mat, scale, out, got, made, *sems):
    local_sem, first_send, first_recv, second_send, second_recv, own_sem = sems
    chunks = src.shape[-1] // width
    me = [lax.axis_index(axis) for axis in axes]
    barrier = pltpu.get_barrier_semaphore()
    for axis, place, n in zip(axes, me, counts):
        for s in range(1, n):
            pl.semaphore_signal(
                barrier, inc=1, device_id={axis: lax.rem(place + s, n)}, device_id_type=MESH
            )
    pl.semaphore_wait(barrier, counts[0] + counts[1] - 2)

    def columns(c):
        return pl.ds(c * width, width)

    def part(c, place):
        return src.at[:, columns(c)] if kind == "gather" else src.at[place, :, columns(c)]

    def first(c, s, place):
        peer = lax.rem(me[0] + s, counts[0])
        return pltpu.make_async_remote_copy(
            src_ref=part(c, peer),
            dst_ref=got.at[place, :, columns(c)],
            send_sem=first_send.at[c, s - 1],
            recv_sem=first_recv.at[c, s - 1],
            device_id={axes[0]: peer},
            device_id_type=MESH,
        )

    def second(c, s, place):
        peer = lax.rem(me[1] + s, counts[1])
        return pltpu.make_async_remote_copy(
            src_ref=made.at[peer, :, columns(c)],
            dst_ref=out.at[place, :, columns(c)],
            send_sem=second_send.at[c, s - 1],
            recv_sem=second_recv.at[c, s - 1],
            device_id={axes[1]: peer},
            device_id_type=MESH,
        )

    sent = []
    kept = []
    for c in range(chunks):
        for s in range(1, counts[0]):
            copy = first(c, s, me[0])
            copy.start()
            sent.append(copy)
        copy = pltpu.make_async_copy(
            part(c, me[0]), got.at[me[0], :, columns(c)], local_sem.at[c]
        )
        copy.start()
        kept.append(copy)
    for c in range(chunks):
        kept[c].wait()
        for s in range(1, counts[0]):
            first(c, s, lax.rem(me[0] - s + counts[0], counts[0])).wait_recv()
        rows = got[:, :, columns(c)].reshape(-1, width)
        term = jnp.dot(mat[...], rows, preferred_element_type=jnp.float32)
        term = (term * scale[...]).astype(jnp.bfloat16)
        made[:, :, columns(c)] = term.reshape(made.shape[0], made.shape[1], width)
        for s in range(1, counts[1]):
            copy = second(c, s, me[1])
            copy.start()
            sent.append(copy)
        copy = pltpu.make_async_copy(
            made.at[me[1], :, columns(c)], out.at[me[1], :, columns(c)], own_sem.at[c]
        )
        copy.start()
        kept.append(copy)
    for c in range(chunks):
        kept[chunks + c].wait()
        for s in range(1, counts[1]):
            second(c, s, lax.rem(me[1] - s + counts[1], counts[1])).wait_recv()
    for copy in sent:
        copy.wait_send()


def relay(axes, collective_id, kind, width, src, mat, scale):
    counts = [lax.axis_size(axis) for axis in axes]
    rows, total = src.shape[-2:]
    out_shape = (counts[1], mat.shape[0] // counts[1], total)
    chunks = total // width
    vmem = pl.BlockSpec(memory_space=pltpu.VMEM)
    return pl.pallas_call(
        functools.partial(relay_kernel, axes, counts, kind, width),
        out_shape=jax.ShapeDtypeStruct(out_shape, jnp.bfloat16),
        in_specs=[pl.BlockSpec(memory_space=pl.ANY), vmem, vmem],
        out_specs=pl.BlockSpec(memory_space=pl.ANY),
        scratch_shapes=[
            pltpu.VMEM((counts[0], rows, total), jnp.bfloat16),
            pltpu.VMEM(out_shape, jnp.bfloat16),
            pltpu.SemaphoreType.DMA((chunks,)),
            pltpu.SemaphoreType.DMA((chunks, counts[0] - 1)),
            pltpu.SemaphoreType.DMA((chunks, counts[0] - 1)),
            pltpu.SemaphoreType.DMA((chunks, counts[1] - 1)),
            pltpu.SemaphoreType.DMA((chunks, counts[1] - 1)),
            pltpu.SemaphoreType.DMA((chunks,)),
        ],
        compiler_params=pltpu.CompilerParams(
            collective_id=collective_id, has_side_effects=True, vmem_limit_bytes=40 * 2**20
        ),
    )(src, mat, scale)


def dot_bt(a, b):
    return lax.dot_general(a, b, (((1,), (1,)), ((), ())), preferred_element_type=jnp.float32)


def expert_kernel(rows_ref, gate_ref, up_ref, down_ref, out_ref, x_ref, g_ref, acc_ref):
    step = pl.program_id(0)

    @pl.when(step == 0)
    def _():
        pair = rows_ref.shape[1]
        depth = pair // 2
        for p in range(rows_ref.shape[0] // 2):
            one = rows_ref[2 * p].astype(jnp.float32)
            two = rows_ref[2 * p + 1].astype(jnp.float32)
            for ref, cut in ((x_ref, slice(0, depth)), (g_ref, slice(depth, pair))):
                ref[p * pair : (p + 1) * pair, :] = jnp.concatenate(
                    [one[cut], two[cut]], axis=0
                ).astype(jnp.bfloat16)

    gate_mat = gate_ref[0]
    up_mat = up_ref[0]
    gate_pre = jnp.dot(x_ref[...], gate_mat, preferred_element_type=jnp.float32)
    up_pre = jnp.dot(x_ref[...], up_mat, preferred_element_type=jnp.float32)
    hidden_grad = dot_bt(g_ref[...], down_ref[0])
    gate_sig = 1.0 / (1.0 + jnp.exp(-gate_pre))
    gate_grad = (hidden_grad * up_pre * gate_sig * (1.0 + gate_pre * (1.0 - gate_sig))).astype(
        jnp.bfloat16
    )
    up_grad = (hidden_grad * gate_pre * gate_sig).astype(jnp.bfloat16)
    term = dot_bt(gate_grad, gate_mat) + dot_bt(up_grad, up_mat)

    @pl.when(step == 0)
    def _():
        acc_ref[...] = term

    @pl.when(step > 0)
    def _():
        acc_ref[...] += term

    @pl.when(step == pl.num_programs(0) - 1)
    def _():
        count, _, half = out_ref.shape
        rows = acc_ref.shape[0] // count
        for d in range(count):
            part = acc_ref[d * rows : (d + 1) * rows, :]
            out_ref[d] = jnp.concatenate([part[:, :half], part[:, half:]], axis=0).astype(
                jnp.bfloat16
            )


def expert_rows(arrived, gate, up, down):
    count, depth, features = arrived.shape
    rows = count * depth // 2
    hidden = gate.shape[2]
    tile = next((t for t in (384, 256, 128) if hidden % t == 0), hidden)
    out_shape = (count, depth, features // 2)
    return pl.pallas_call(
        expert_kernel,
        grid=(hidden // tile,),
        out_shape=jax.ShapeDtypeStruct(out_shape, jnp.bfloat16),
        in_specs=[
            pl.BlockSpec(arrived.shape, lambda f: (0, 0, 0)),
            pl.BlockSpec((1, features, tile), lambda f: (0, 0, f)),
            pl.BlockSpec((1, features, tile), lambda f: (0, 0, f)),
            pl.BlockSpec((1, tile, features), lambda f: (0, f, 0)),
        ],
        out_specs=pl.BlockSpec(out_shape, lambda f: (0, 0, 0)),
        scratch_shapes=[
            pltpu.VMEM((rows, features), jnp.bfloat16),
            pltpu.VMEM((rows, features), jnp.bfloat16),
            pltpu.VMEM((rows, features), jnp.float32),
        ],
        compiler_params=pltpu.CompilerParams(vmem_limit_bytes=60 * 2**20),
    )(arrived, gate, up, down)


def normalize(residual, norm_gain):
    residual_f = residual.astype(jnp.float32)
    factor = lax.rsqrt(jnp.mean(residual_f * residual_f, axis=-1, keepdims=True) + 1e-05)
    return (residual_f, factor, (residual_f * factor * norm_gain).astype(jnp.bfloat16))


def block_terms(key_part, value_part, log_steps):
    place = jnp.arange(log_steps.shape[0], dtype=jnp.int32)
    levels = jnp.sum(
        jnp.where(place[:, None] >= place[None, :], log_steps[None, :], 0.0), axis=1
    )
    block_total = levels[-1]
    to_end = jnp.exp(block_total - levels)
    key_state = lax.dot_general(
        key_part.astype(jnp.float32) * to_end[:, None],
        value_part.astype(jnp.float32),
        (((0,), (0,)), ((), ())),
        precision=lax.Precision.HIGHEST,
    )
    return (levels, block_total, key_state)


def block_grads(
    query_part, key_part, value_part, grad_part, levels, state_in, adjoint_out, score_scale
):
    block_total = levels[-1]
    from_start = jnp.exp(levels)
    to_end = jnp.exp(block_total - levels)
    token_position = jnp.arange(levels.shape[0], dtype=jnp.int32)
    causal = token_position[:, None] >= token_position[None, :]
    fading = jnp.exp(jnp.where(causal, levels[:, None] - levels[None, :], -jnp.inf))
    scores = lax.dot_general(
        query_part, key_part, (((1,), (1,)), ((), ())), preferred_element_type=jnp.float32
    )
    attn_probs = (score_scale * scores * fading).astype(jnp.bfloat16)
    grad_scores = lax.dot_general(
        grad_part, value_part, (((1,), (1,)), ((), ())), preferred_element_type=jnp.float32
    )
    pull_weights = (score_scale * grad_scores * fading).astype(jnp.bfloat16)
    grad_f = grad_part.astype(jnp.float32)
    query_out = jnp.dot(pull_weights, key_part, preferred_element_type=jnp.float32)
    query_out = query_out + score_scale * from_start[:, None] * lax.dot_general(
        grad_f, state_in, (((1,), (1,)), ((), ())), precision=lax.Precision.HIGHEST
    )
    key_out = lax.dot_general(
        pull_weights, query_part, (((0,), (0,)), ((), ())), preferred_element_type=jnp.float32
    )
    key_out = key_out + to_end[:, None] * lax.dot_general(
        value_part.astype(jnp.float32),
        adjoint_out,
        (((1,), (1,)), ((), ())),
        precision=lax.Precision.HIGHEST,
    )
    value_out = lax.dot_general(
        attn_probs, grad_part, (((0,), (0,)), ((), ())), preferred_element_type=jnp.float32
    )
    value_out = value_out + to_end[:, None] * jnp.dot(
        key_part.astype(jnp.float32), adjoint_out, precision=lax.Precision.HIGHEST
    )
    return (
        query_out.astype(jnp.bfloat16),
        key_out.astype(jnp.bfloat16),
        value_out.astype(jnp.bfloat16),
    )


def body(
    query_rows,
    key_rows,
    value_rows,
    log_decay,
    residual,
    norm_gain,
    out_grad,
    experts_of,
    route_weight,
    output_weight,
    expert_gate,
    expert_up,
    expert_down,
):
    ctx_count = lax.axis_size("ctx")
    exp_count = lax.axis_size("exp")
    ctx_place = lax.axis_index("ctx")
    token_count = residual.shape[0]
    features = residual.shape[1]
    half = features // 2
    capacity = max(2, 3 * token_count // exp_count)
    depth = -(-ctx_count * capacity // 8) * 8
    slots = exp_count * depth
    all_tokens = ctx_count * token_count

    residual_f, factor, expert_input = normalize(residual, norm_gain)
    levels, block_total, key_state = block_terms(key_rows, value_rows, log_decay[0])
    meta = jnp.concatenate(
        [
            experts_of.T.astype(jnp.float32),
            route_weight.T,
            jnp.broadcast_to(block_total, (1, token_count)),
        ],
        axis=0,
    )
    meta = jnp.pad(meta, ((0, 3), (0, 128 - token_count)))
    metas, key_states = exchange("ctx", 0, [meta, key_state.astype(jnp.bfloat16)], ("gather", "gather"))

    choice = metas[:, 0:2, :token_count].astype(jnp.int32)
    choice_by_token = jnp.transpose(choice, (0, 2, 1)).reshape(-1)
    weights = jnp.transpose(metas[:, 2:4, :token_count], (0, 2, 1)).reshape(-1)
    order = jnp.arange(2 * all_tokens, dtype=jnp.int32)
    ahead = (choice_by_token[:, None] == choice_by_token[None, :]) & (
        order[:, None] > order[None, :]
    )
    target = choice_by_token * depth + jnp.sum(ahead, axis=1, dtype=jnp.int32)
    slot_ids = jnp.arange(slots, dtype=jnp.int32)
    hits = (slot_ids[:, None] == target[None, :]).astype(jnp.float32)
    slot_weight = jnp.sum(hits * weights[None, :], axis=1)
    pick = jnp.sum(hits.reshape(exp_count, depth, ctx_count, token_count, 2), axis=-1)
    none = jnp.zeros_like(pick)
    pick_both = jnp.concatenate(
        [
            jnp.concatenate([pick, none], axis=3),
            jnp.concatenate([none, pick], axis=3),
        ],
        axis=1,
    ).reshape(2 * slots, 2 * all_tokens)
    row_scale = jnp.concatenate(
        [jnp.ones((exp_count, depth), jnp.float32), slot_weight.reshape(exp_count, depth)], axis=1
    )
    arrived = relay(
        ("ctx", "exp"),
        1,
        "gather",
        features // 6,
        jnp.concatenate([expert_input, out_grad], axis=0),
        pick_both.astype(jnp.bfloat16),
        row_scale.reshape(-1, 1),
    )
    partials = expert_rows(arrived, expert_gate, expert_up, expert_down)

    back = jnp.transpose(pick, (2, 3, 0, 1))[:, None, :, :, None, :]
    halves = jnp.eye(2, dtype=jnp.float32)[None, :, None, None, :, None]
    merge = (back * halves).reshape(2 * all_tokens, 2 * slots).astype(jnp.bfloat16)
    groups = relay(
        ("exp", "ctx"),
        2,
        "swap",
        half // 4,
        partials,
        merge,
        jnp.ones((2 * all_tokens, 1), jnp.float32),
    )

    def split(a):
        return jnp.stack([a[:, :half], a[:, half:]], axis=0)

    moe_grad = jnp.sum(groups.astype(jnp.float32), axis=0).reshape(2, token_count, half)
    scaled = norm_gain.reshape(2, 1, half) * moe_grad
    unit_rows = split(residual_f * factor)
    mean = jnp.sum(unit_rows * scaled, axis=(0, 2), keepdims=True) * (1.0 / features)
    total_grad = split(out_grad.astype(jnp.float32)) + factor[None] * (scaled - unit_rows * mean)
    resid_grad = total_grad.astype(jnp.bfloat16).reshape(2 * token_count, half)
    [resid_all] = exchange("exp", 4, [resid_grad], ("gather",))
    resid_all = resid_all.reshape(exp_count, 2, token_count, half)
    block_len = query_rows.shape[0]
    head_size = query_rows.shape[1]
    attn_grad = (
        dot_bt(resid_all[:, 0].reshape(block_len, half), output_weight[:, :half])
        + dot_bt(resid_all[:, 1].reshape(block_len, half), output_weight[:, half:])
    ).astype(jnp.bfloat16)
    score_scale = 1.0 / math.sqrt(head_size * block_len * ctx_count)
    adjoint = score_scale * lax.dot_general(
        query_rows.astype(jnp.float32) * jnp.exp(levels)[:, None],
        attn_grad.astype(jnp.float32),
        (((0,), (0,)), ((), ())),
        precision=lax.Precision.HIGHEST,
    )
    [adjoints] = exchange("ctx", 5, [adjoint.astype(jnp.bfloat16)], ("gather",))

    totals = metas[:, 4, 0]
    place = jnp.arange(ctx_count, dtype=jnp.int32)
    between = (place[None, :] > jnp.minimum(place, ctx_place)[:, None]) & (
        place[None, :] < jnp.maximum(place, ctx_place)[:, None]
    )
    decay = jnp.exp(jnp.sum(jnp.where(between, totals[None, :], 0.0), axis=1))
    before = jnp.where(place < ctx_place, decay, 0.0)
    after = jnp.where(place > ctx_place, decay, 0.0)
    state_in = jnp.sum(before[:, None, None] * key_states.astype(jnp.float32), axis=0)
    adjoint_out = jnp.sum(after[:, None, None] * adjoints.astype(jnp.float32), axis=0)
    return block_grads(
        query_rows, key_rows, value_rows, attn_grad, levels, state_in, adjoint_out, score_scale
    )


def solution(mesh):
    placed = (
        P("ctx", "exp"),
        P("ctx", "exp"),
        P("ctx", "exp"),
        P("exp", "ctx"),
        P(("ctx", "exp"), None),
        P(),
        P(("ctx", "exp"), None),
        P(("ctx", "exp"), None),
        P(("ctx", "exp"), None),
        P("exp", None),
        P("exp", None, "ctx"),
        P("exp", None, "ctx"),
        P("exp", "ctx", None),
    )
    return jax.shard_map(
        body,
        mesh=mesh,
        in_specs=placed,
        out_specs=(P("ctx", "exp"), P("ctx", "exp"), P("ctx", "exp")),
        check_vma=False,
    )
```
